512 devices in a mesh: grp: 16 (over z_lo, y), dev: 32 (over x, z_hi, core).
Axes of the slice: x: 4, y: 4, z: 16 (z_hi: 4, z_lo: 4; z = z_hi * 4 + z_lo), core: 2. Of those that a mesh axis runs over, the one named last changes fastest.
Arguments:
- spectra: bfloat16 [2, 256, 2048, 384], P(None, None, ('grp', 'dev')), may hold values from -6 to 6
- validity: int32 [2048, 384], P(('grp', 'dev')), may hold values 0 or 1
Outputs:
- correlations: float32 [4, 2048, 128, 128], P(None, ('grp', 'dev'))
The draws below stay inside these ranges and needn't reach their ends.
All inputs are finite; a program needn't handle non-finite values. No bound on the sum of `validity` on one device may be relied on, other than what follows from the above.
Results may differ from the reference program's by a relative error of at most 0.004.
Values may be sent and summed in bfloat16 or wider, within the bound.
A program may use at most 64 MiB of HBM per device.

```python
import jax
import jax.numpy as jnp
from jax import lax

F = 256
LAGS = 128
W = 384
ROUNDS = 4
CG = 128
C = 2048


def set_ends(array, key, smallest, largest):
    longest = array.shape.index(max(array.shape))
    spots = []
    for shift in (0, 1):
        where = [jax.random.randint(jax.random.fold_in(key, axis), (), 0, length) for axis, length in enumerate(array.shape)]
        where[longest] = (where[longest] + shift) % array.shape[longest]
        spots.append(tuple(where))
    return array.at[spots[0]].set(smallest).at[spots[1]].set(largest)


def shard_levels(stream_key, shape, shards, smallest, largest):
    loudness = 1.0
    for position, blocks in shards:
        heights = jax.random.uniform(jax.random.fold_in(jax.random.fold_in(stream_key, 6), position), (blocks,), jnp.float32, smallest / len(shards), largest / len(shards))
        loudness = loudness * jnp.repeat(jnp.exp(heights), shape[position] // blocks).reshape((-1,) + (1,) * (len(shape) - 1 - position))
    return loudness


def noise(rng, extent, scale, reach, split=(), kind=jnp.bfloat16):
    entries = jax.random.normal(rng, extent, jnp.float32) * scale
    if len(split) > 0:
        entries = shard_levels(rng, extent, split, -0.22, 0.18) * entries
    return jnp.clip(entries, min=-reach, max=reach).astype(kind)


def setup_inputs(seed: int = 0) -> dict:
    seeds = jax.random.split(jax.random.key(seed), 3)
    spectra = noise(seeds[0], (2, F, C, W), 1.0, 6.0, ((2, 512),))
    validity = set_ends((jax.random.randint(seeds[1], (C, W), 0, 8) < 7).astype(jnp.int32), jax.random.fold_in(seeds[1], 1), 0, 1)
    return {"spectra": spectra, "validity": validity}


def lag_tables():
    freq = jnp.arange(F, dtype=jnp.int32)[:, None]
    lag = jnp.arange(LAGS, dtype=jnp.int32)[None, :] - LAGS // 2
    phase = jnp.mod(freq * lag, 2 * F).astype(jnp.float32)
    angle = jnp.pi * phase / F
    return (jnp.cos(angle), jnp.sin(angle))

def reference(spectra, validity):
    groups = C // CG
    cosine, sine = lag_tables()
    norm_factor = 1.0 / jnp.sqrt(jnp.float32(W) * F)

    def whiten(group_number):
        start = group_number * CG
        block = lax.dynamic_slice_in_dim(spectra, start, CG, 2).astype(jnp.float32)
        live = lax.dynamic_slice_in_dim(validity, start, CG, 0).astype(jnp.float32)
        masked = block * live[None, None, :, :]
        power_mean = lax.optimization_barrier(jnp.sum(masked * masked, axis=(0, 3))) / W + 1e-06
        return (masked / jnp.sqrt(power_mean)[None, :, :, None]).astype(jnp.bfloat16)
    whitened = lax.map(whiten, jnp.arange(groups, dtype=jnp.int32))
    outputs = []
    for offset in range(ROUNDS):

        def one_group(group_number):
            own = whitened[group_number].astype(jnp.float32)
            other = whitened[jnp.mod(group_number - offset, groups)].astype(jnp.float32)
            real_part = jnp.einsum('fiw,fjw->fij', own[0], other[0]) + jnp.einsum('fiw,fjw->fij', own[1], other[1])
            imag_part = jnp.einsum('fiw,fjw->fij', own[1], other[0]) - jnp.einsum('fiw,fjw->fij', own[0], other[1])
            real_part = real_part.astype(jnp.bfloat16).astype(jnp.float32)
            imag_part = imag_part.astype(jnp.bfloat16).astype(jnp.float32)
            lagged = jnp.einsum('fij,ft->ijt', real_part, cosine, precision=lax.Precision.HIGHEST)
            lagged = lagged - jnp.einsum('fij,ft->ijt', imag_part, sine, precision=lax.Precision.HIGHEST)
            return lagged * norm_factor
        result = lax.map(one_group, jnp.arange(groups, dtype=jnp.int32))
        outputs.append(result.reshape(C, CG, LAGS))
    return jnp.stack(outputs, axis=0)
```

```python
import functools

import jax
import jax.numpy as jnp
import numpy as np
from jax import lax
from jax.experimental import pallas as pl
from jax.experimental.pallas import tpu as pltpu
from jax.sharding import PartitionSpec as P

MESH = pl.DeviceIdType.MESH
FREQS = 256
LAGS = 128
ROUNDS = 4
WINDOWS = 384
GROUP = 128
PEERS = 32
PARTS = 2
SUB = 2
FSUB = FREQS // PEERS // SUB
OWN = GROUP // PEERS
ROWS = OWN * FSUB
LANES = 128


def lag_table():
    freq = np.arange(FREQS, dtype=np.int64)[:, None]
    lag = np.arange(LAGS, dtype=np.int64)[None, :] - LAGS // 2
    angle = np.pi * np.mod(freq * lag, 2 * FREQS) / FREQS
    signed = np.stack([np.cos(angle), -np.sin(angle)], axis=0).astype(np.float32)
    upper = signed.astype(jnp.bfloat16)
    lower = (signed - upper.astype(np.float32)).astype(jnp.bfloat16)
    split = np.stack([upper, lower], axis=0)
    split = split.reshape(2, PARTS, PEERS, SUB, FSUB, LAGS)
    split = split.transpose(3, 2, 1, 4, 0, 5)
    table = np.zeros((SUB, PEERS, 2, PARTS, FSUB, 2, 2, LAGS), dtype=jnp.bfloat16)
    for pair in range(2):
        table[:, :, pair, :, :, :, pair, :] = split
    return table.reshape(SUB, PEERS * 2 * PARTS * FSUB, 4 * LAGS)


def kernel(x_ref, mask_ref, table_ref, out_ref, send, recv, spread, blocks, left, terms, back, home,
           send_sem, recv_sem, ring_send, ring_recv, back_send, back_recv, self_sem):
    grp = lax.axis_index("grp")
    dev = lax.axis_index("dev")
    z_lo, y = grp // 4, grp % 4
    x, z_hi, core = dev // 8, (dev // 2) % 4, dev % 2
    plane = z_hi * 4 + z_lo
    chunk = plane * 2 + core
    alone = x == z_lo

    def worker(q):
        return ((q // 2) % 4 * 4 + y, z_lo * 8 + q // 8 * 2 + q % 2)

    def owner(s):
        return (x * 4 + y, s)

    def ring(by):
        g = (x * 4 + y + by + 16) % 16
        return (z_lo * 4 + g % 4, g // 4 * 8 + z_hi * 2 + core)

    barrier = pltpu.get_barrier_semaphore()

    def greet(i, _):
        @pl.when(jnp.logical_not(jnp.logical_and(alone, i == chunk)))
        def _():
            pl.semaphore_signal(barrier, inc=1, device_id=worker(i), device_id_type=MESH)

        @pl.when(jnp.logical_not(jnp.logical_and(alone, i == dev)))
        def _():
            pl.semaphore_signal(barrier, inc=1, device_id=owner(i), device_id_type=MESH)

        return 0

    lax.fori_loop(0, PEERS, greet, 0)
    for by in (1, -1, 3, -3):
        pl.semaphore_signal(barrier, inc=1, device_id=ring(by), device_id_type=MESH)

    def whiten(k, q):
        masked = x_ref[q * SUB + k].astype(jnp.float32) * mask_ref[...][None]
        power = jnp.sum(jnp.sum(masked * masked, axis=0), axis=1, keepdims=True) / WINDOWS + 1e-06
        send[k, q] = (masked / jnp.sqrt(power)[None]).astype(jnp.bfloat16)

    def in_copy(k, q, s):
        return pltpu.make_async_remote_copy(
            src_ref=send.at[k, q], dst_ref=recv.at[k, s], send_sem=send_sem.at[k, q],
            recv_sem=recv_sem.at[k, s], device_id=worker(q), device_id_type=MESH)

    def in_self(k):
        return pltpu.make_async_copy(send.at[k, chunk], recv.at[k, dev], self_sem.at[k])

    def nth(n):
        step = n // 2
        off = lax.select(step % 2 == 0, 8 - step // 2, step // 2 - 7)
        return (plane + off + 16) % 16 * 2 + (core + n) % 2

    def send_in(k, q):
        here = jnp.logical_and(alone, q == chunk)

        @pl.when(jnp.logical_not(here))
        def _():
            in_copy(k, q, dev).start()

        @pl.when(here)
        def _():
            in_self(k).start()

    def first(n, _):
        whiten(0, nth(n))
        return 0

    lax.fori_loop(0, PEERS, first, 0)
    total = 2 * PEERS + 4 - 2 * alone.astype(jnp.int32)
    pl.semaphore_wait(barrier, total)

    def first_send(n, _):
        send_in(0, nth(n))
        return 0

    lax.fori_loop(0, PEERS, first_send, 0)

    def second(n, _):
        whiten(1, nth(n))
        send_in(1, nth(n))
        return 0

    lax.fori_loop(0, PEERS, second, 0)

    def wait_in(k):
        def body(s, _):
            here = jnp.logical_and(alone, s == dev)

            @pl.when(jnp.logical_not(here))
            def _():
                in_copy(k, s, s).wait_recv()

            @pl.when(here)
            def _():
                in_self(k).wait()

            return 0

        lax.fori_loop(0, PEERS, body, 0)

    def regroup(k):
        for part in range(PARTS):
            for w in range(WINDOWS // LANES):
                spread[w] = recv[k, :, part, :, w * LANES:(w + 1) * LANES].astype(jnp.float32).reshape(
                    PEERS * ROWS, LANES)
            for f in range(FSUB):
                for w in range(WINDOWS // LANES):
                    at = part * WINDOWS + w * LANES
                    blocks[k, 0, f, :, at:at + LANES] = spread[
                        w, pl.ds(f, GROUP, stride=FSUB), :].astype(jnp.bfloat16)

    half = FSUB // 2

    def ring_copy(k, which):
        by, src, dst = (
            (1, blocks.at[k, 0], blocks.at[k, 1]),
            (3, blocks.at[k, 0], blocks.at[k, 3]),
            (1, blocks.at[k, 1, 0:half], blocks.at[k, 2, 0:half]),
            (-1, blocks.at[k, 3, half:FSUB], blocks.at[k, 2, half:FSUB]),
        )[which]
        return pltpu.make_async_remote_copy(
            src_ref=src, dst_ref=dst, send_sem=ring_send.at[k, which], recv_sem=ring_recv.at[k, which],
            device_id=ring(by), device_id_type=MESH)

    def exchange(k):
        wait_in(k)
        regroup(k)
        ring_copy(k, 0).start()
        ring_copy(k, 1).start()

    def cross(k):
        def body(f, _):
            own = blocks[k, 0, f]
            first_part, second_part = own[:, :WINDOWS], own[:, WINDOWS:]
            left[0:GROUP, :] = own
            left[GROUP:, 0:WINDOWS] = second_part
            left[GROUP:, WINDOWS:] = -first_part
            for r in range(ROUNDS):
                product = lax.dot_general(
                    left[...], blocks[k, r, f], (((1,), (1,)), ((), ())), preferred_element_type=jnp.float32)
                for part in range(PARTS):
                    terms[r, pl.ds(part * FSUB + f, GROUP, stride=PARTS * FSUB), :] = product[
                        part * GROUP:(part + 1) * GROUP]
            return 0

        lax.fori_loop(0, FSUB, body, 0)
        for r in range(ROUNDS):
            back[k, :, r] = terms[r].astype(jnp.bfloat16).reshape(PEERS, OWN * PARTS * FSUB, LANES)

    def out_copy(k, s, q):
        return pltpu.make_async_remote_copy(
            src_ref=back.at[k, s], dst_ref=home.at[k, q], send_sem=back_send.at[k, s],
            recv_sem=back_recv.at[k, q], device_id=owner(s), device_id_type=MESH)

    def out_self(k):
        return pltpu.make_async_copy(back.at[k, dev], home.at[k, chunk], self_sem.at[SUB + k])

    def send_out(k):
        def body(n, _):
            step = n // 8
            s = (n // 2) % 4 * 8 + (z_hi + 2 + 2 * (step % 2) + step // 2) % 4 * 2 + (core + n) % 2
            here = jnp.logical_and(alone, s == dev)

            @pl.when(jnp.logical_not(here))
            def _():
                out_copy(k, s, chunk).start()

            @pl.when(here)
            def _():
                out_self(k).start()

            return 0

        lax.fori_loop(0, PEERS, body, 0)

    def forward(k):
        ring_copy(k, 0).wait_recv()
        ring_copy(k, 2).start()
        ring_copy(k, 1).wait_recv()
        ring_copy(k, 3).start()
        ring_copy(k, 2).wait_recv()
        ring_copy(k, 3).wait_recv()

    def wait_out(k):
        def body(q, _):
            here = jnp.logical_and(alone, q == chunk)

            @pl.when(jnp.logical_not(here))
            def _():
                out_copy(k, q, q).wait_recv()

            @pl.when(here)
            def _():
                out_self(k).wait()

            return 0

        lax.fori_loop(0, PEERS, body, 0)

    scale = 1.0 / np.sqrt(np.float32(WINDOWS) * FREQS)

    def to_lags(k):
        def body(n, _):
            r, pair = n // 2, n % 2
            rows = pl.multiple_of(pair * 16, 16)
            values = home[k, :, r, pl.ds(rows, 16), :].reshape(PEERS * 16, LANES)
            both = lax.dot_general(
                values, table_ref[k], (((0,), (0,)), ((), ())), preferred_element_type=jnp.float32)
            lagged = (both[:, :2 * LAGS] + both[:, 2 * LAGS:]) * scale
            for c in range(2):
                piece = lagged[:, c * LAGS:(c + 1) * LAGS]
                if k == 0:
                    out_ref[r, pair * 2 + c] = piece
                else:
                    out_ref[r, pair * 2 + c] += piece
            return 0

        lax.fori_loop(0, ROUNDS * 2, body, 0)

    for k in range(SUB):
        exchange(k)
        forward(k)
        cross(k)
        send_out(k)
    for k in range(SUB):
        wait_out(k)
        to_lags(k)

    for k in range(SUB):
        for which in range(4):
            ring_copy(k, which).wait_send()

        def finish(n, _):
            @pl.when(jnp.logical_not(jnp.logical_and(alone, n == chunk)))
            def _():
                in_copy(k, n, dev).wait_send()

            @pl.when(jnp.logical_not(jnp.logical_and(alone, n == dev)))
            def _():
                out_copy(k, n, chunk).wait_send()

            return 0

        lax.fori_loop(0, PEERS, finish, 0)


def local(spectra, validity):
    pieces = spectra.reshape(PARTS, PEERS * SUB, FSUB, OWN, WINDOWS).transpose(1, 0, 3, 2, 4)
    pieces = pieces.reshape(PEERS * SUB, PARTS, ROWS, WINDOWS)
    mask = jnp.repeat(validity.astype(jnp.float32), FSUB, axis=0)
    table = jnp.asarray(lag_table())
    vmem = pl.BlockSpec(memory_space=pltpu.VMEM)
    dma = pltpu.SemaphoreType.DMA
    return pl.pallas_call(
        kernel,
        out_shape=jax.ShapeDtypeStruct((ROUNDS, OWN, GROUP, LAGS), jnp.float32),
        in_specs=[vmem, vmem, vmem],
        out_specs=vmem,
        scratch_shapes=[
            pltpu.VMEM((SUB, PEERS, PARTS, ROWS, WINDOWS), jnp.bfloat16),
            pltpu.VMEM((SUB, PEERS, PARTS, ROWS, WINDOWS), jnp.bfloat16),
            pltpu.VMEM((WINDOWS // LANES, PEERS * ROWS, LANES), jnp.float32),
            pltpu.VMEM((SUB, ROUNDS, FSUB, GROUP, PARTS * WINDOWS), jnp.bfloat16),
            pltpu.VMEM((2 * GROUP, PARTS * WINDOWS), jnp.bfloat16),
            pltpu.VMEM((ROUNDS, GROUP * PARTS * FSUB, LANES), jnp.float32),
            pltpu.VMEM((SUB, PEERS, ROUNDS, OWN * PARTS * FSUB, LANES), jnp.bfloat16),
            pltpu.VMEM((SUB, PEERS, ROUNDS, OWN * PARTS * FSUB, LANES), jnp.bfloat16),
            dma((SUB, PEERS)), dma((SUB, PEERS)),
            dma((SUB, 4)), dma((SUB, 4)),
            dma((SUB, PEERS)), dma((SUB, PEERS)),
            dma((2 * SUB,)),
        ],
        compiler_params=pltpu.CompilerParams(
            collective_id=1, has_side_effects=True, vmem_limit_bytes=48 << 20),
        name="correlate",
    )(pieces, mask, table)


def solution(mesh):
    in_specs = (P(None, None, ("grp", "dev"), None), P(("grp", "dev"), None))
    out_specs = P(None, ("grp", "dev"), None, None)
    return jax.shard_map(local, mesh=mesh, in_specs=in_specs, out_specs=out_specs, check_vma=False)
```

```python
import jax
import jax.numpy as jnp
import numpy as np
from jax import lax
from jax.experimental import pallas as pl
from jax.experimental.pallas import tpu as pltpu
from jax.sharding import PartitionSpec as P

MESH = pl.DeviceIdType.MESH
FREQS = 256
LAGS = 128
ROUNDS = 4
WINDOWS = 384
GROUP = 128
PEERS = 32
PARTS = 2
SUB = 2
FSUB = FREQS // PEERS // SUB
OWN = GROUP // PEERS
ROWS = OWN * FSUB
BACK_ROWS = OWN * PARTS * FSUB
LANES = 128
BATCH = 4


def lag_table():
    freq = np.arange(FREQS, dtype=np.int64)[:, None]
    lag = np.arange(LAGS, dtype=np.int64)[None, :] - LAGS // 2
    angle = np.pi * np.mod(freq * lag, 2 * FREQS) / FREQS
    signed = np.stack([np.cos(angle), -np.sin(angle)], axis=0).astype(np.float32)
    upper = signed.astype(jnp.bfloat16)
    lower = (signed - upper.astype(np.float32)).astype(jnp.bfloat16)
    split = np.stack([upper, lower], axis=0)
    split = split.reshape(2, PARTS, PEERS, SUB, FSUB, LAGS)
    split = split.transpose(3, 2, 1, 4, 0, 5)
    table = np.zeros((SUB, PEERS, 2, PARTS, FSUB, 2, 2, LAGS), dtype=jnp.bfloat16)
    for pair in range(2):
        table[:, :, pair, :, :, :, pair, :] = split
    return table.reshape(SUB, PEERS * 2 * PARTS * FSUB, 4 * LAGS)


def kernel(x_ref, mask_ref, table_ref, out_ref, send, recv, spread, blocks, carry, left, terms, loan, back, home,
           send_sem, recv_sem, ring_send, ring_recv, back_send, back_recv, self_sem):
    grp = lax.axis_index("grp")
    dev = lax.axis_index("dev")
    z_lo, y = grp // 4, grp % 4
    x, z_hi, core = dev // 8, (dev // 2) % 4, dev % 2
    plane = z_hi * 4 + z_lo
    chunk = plane * 2 + core
    flip = 1 - 2 * (z_lo % 2)
    held = (z_lo + flip * x + 4) % 4
    alone = x == 0

    def worker(q):
        at = q // 2
        column = ((z_lo - at) * (1 - 2 * (at % 2)) + 32) % 4
        return (at % 4 * 4 + y, column * 8 + at // 4 * 2 + q % 2)

    def owner(s):
        return (held * 4 + y, s)

    def ring(by):
        g = (held * 4 + y + by + 16) % 16
        column = ((g // 4 - z_lo) * flip + 8) % 4
        return (z_lo * 4 + g % 4, column * 8 + z_hi * 2 + core)

    barrier = pltpu.get_barrier_semaphore()

    def greet(i, _):
        @pl.when(jnp.logical_not(jnp.logical_and(alone, i == chunk)))
        def _():
            pl.semaphore_signal(barrier, inc=1, device_id=worker(i), device_id_type=MESH)

        @pl.when(jnp.logical_not(jnp.logical_and(alone, i == dev)))
        def _():
            pl.semaphore_signal(barrier, inc=1, device_id=owner(i), device_id_type=MESH)

        return 0

    lax.fori_loop(0, PEERS, greet, 0)
    for by in (1, -1, 3, -3, 4, -4):
        pl.semaphore_signal(barrier, inc=1, device_id=ring(by), device_id_type=MESH)

    def whiten(k):
        def body(n, _):
            at = pl.multiple_of(n * BATCH, BATCH)
            masked = x_ref[k, pl.ds(at, BATCH)].astype(jnp.float32) * mask_ref[...][None, None]
            power = jnp.sum(jnp.sum(masked * masked, axis=1, keepdims=True), axis=3, keepdims=True) / WINDOWS + 1e-06
            send[k, pl.ds(at, BATCH)] = (masked / jnp.sqrt(power)).astype(jnp.bfloat16)
            return 0

        lax.fori_loop(0, PEERS // BATCH, body, 0)

    def in_copy(k, q, s):
        return pltpu.make_async_remote_copy(
            src_ref=send.at[k, q], dst_ref=recv.at[k, s], send_sem=send_sem.at[k, q],
            recv_sem=recv_sem.at[k, s], device_id=worker(q), device_id_type=MESH)

    def in_self(k):
        return pltpu.make_async_copy(send.at[k, chunk], recv.at[k, dev], self_sem.at[k])

    def nth(n):
        step = n // 2
        off = lax.select(step % 2 == 0, 8 - step // 2, step // 2 - 7)
        return (plane + off + 16) % 16 * 2 + (core + n) % 2

    def send_in(k):
        def body(n, _):
            q = nth(n)
            here = jnp.logical_and(alone, q == chunk)

            @pl.when(jnp.logical_not(here))
            def _():
                in_copy(k, q, dev).start()

            @pl.when(here)
            def _():
                in_self(k).start()

            return 0

        lax.fori_loop(0, PEERS, body, 0)

    def wait_in(k):
        def body(s, _):
            here = jnp.logical_and(alone, s == dev)

            @pl.when(jnp.logical_not(here))
            def _():
                in_copy(k, s, s).wait_recv()

            @pl.when(here)
            def _():
                in_self(k).wait()

            return 0

        lax.fori_loop(0, PEERS, body, 0)

    def regroup(k):
        for part in range(PARTS):
            for w in range(WINDOWS // LANES):
                spread[w] = recv[k, :, part, :, w * LANES:(w + 1) * LANES].astype(jnp.float32).reshape(
                    PEERS * ROWS, LANES)
            for f in range(FSUB):
                for w in range(WINDOWS // LANES):
                    at = part * WINDOWS + w * LANES
                    blocks[k, 0, f, :, at:at + LANES] = spread[
                        w, pl.ds(f, GROUP, stride=FSUB), :].astype(jnp.bfloat16)

    def ring_copy(by, src, dst, k, which, f):
        return pltpu.make_async_remote_copy(
            src_ref=src, dst_ref=dst, send_sem=ring_send.at[k, which, f], recv_sem=ring_recv.at[k, which, f],
            device_id=ring(by), device_id_type=MESH)

    def next_copy(k, f):
        return ring_copy(1, blocks.at[k, 0, f], blocks.at[k, 1, f], k, 0, f)

    def third_copy(k, f):
        return ring_copy(3, blocks.at[k, 0, f], blocks.at[k, 2, f], k, 1, f)

    def turn_copy(k, f):
        return ring_copy(-3, blocks.at[k, 0, f], carry.at[k, f], k, 2, f)

    def pass_copy(k, f):
        return ring_copy(4, carry.at[k, f], blocks.at[k, 1, f], k, 0, f)

    def loan_copy(k):
        return ring_copy(-1, loan.at[k], back.at[k, 3], k, 3, 0)

    def send_ring(k):
        for f in range(FSUB):
            @pl.when(y < 3)
            def _():
                next_copy(k, f).start()

            @pl.when(y == 3)
            def _():
                turn_copy(k, f).start()

            third_copy(k, f).start()

    def pass_on(k, f):
        @pl.when(y == 0)
        def _():
            turn_copy(k, f).wait_recv()
            pass_copy(k, f).start()

    def end_ring(k):
        for f in range(FSUB):
            @pl.when(y < 3)
            def _():
                next_copy(k, f).wait_send()

            @pl.when(y == 3)
            def _():
                turn_copy(k, f).wait_send()

            @pl.when(y == 0)
            def _():
                pass_copy(k, f).wait_send()

            third_copy(k, f).wait_send()
        loan_copy(k).wait_send()

    def cross(k, one, other, put, ready):
        def body(f, _):
            ready(f)
            own = blocks[k, one, f]
            left[0:GROUP, :] = own
            left[GROUP:, 0:WINDOWS] = own[:, WINDOWS:]
            left[GROUP:, WINDOWS:] = -own[:, :WINDOWS]
            product = lax.dot_general(
                left[...], blocks[k, other, f], (((1,), (1,)), ((), ())), preferred_element_type=jnp.float32)
            for part in range(PARTS):
                terms[pl.ds(part * FSUB + f, GROUP, stride=PARTS * FSUB), :] = product[
                    part * GROUP:(part + 1) * GROUP]
            return 0

        lax.fori_loop(0, FSUB, body, 0)
        put[...] = terms[...].astype(jnp.bfloat16).reshape(PEERS, BACK_ROWS, LANES)

    def out_refs(k, late, s, q):
        if late:
            return back.at[k, 1:ROUNDS, s], home.at[k, q, 1:ROUNDS]
        return back.at[k, 0, s], home.at[k, q, 0]

    def out_copy(k, late, s, q):
        src, dst = out_refs(k, late, s, q)
        return pltpu.make_async_remote_copy(
            src_ref=src, dst_ref=dst, send_sem=back_send.at[k, late, s],
            recv_sem=back_recv.at[k, late, q], device_id=owner(s), device_id_type=MESH)

    def out_self(k, late):
        src, dst = out_refs(k, late, dev, chunk)
        return pltpu.make_async_copy(src, dst, self_sem.at[SUB + 2 * k + late])

    def send_out(k, late):
        def body(n, _):
            s = (x + n // 4) % 4 * 8 + (z_hi + 2 + n) % 4 * 2 + (core + n // 16) % 2
            here = jnp.logical_and(alone, s == dev)

            @pl.when(jnp.logical_not(here))
            def _():
                out_copy(k, late, s, chunk).start()

            @pl.when(here)
            def _():
                out_self(k, late).start()

            return 0

        lax.fori_loop(0, PEERS, body, 0)

    def wait_out(k):
        def body(q, _):
            here = jnp.logical_and(alone, q == chunk)

            @pl.when(jnp.logical_not(here))
            def _():
                for late in range(2):
                    out_copy(k, late, q, q).wait_recv()

            @pl.when(here)
            def _():
                for late in range(2):
                    out_self(k, late).wait()

            return 0

        lax.fori_loop(0, PEERS, body, 0)

    scale = 1.0 / np.sqrt(np.float32(WINDOWS) * FREQS)

    def to_lags(k):
        def body(n, _):
            slot, pair = n // 2, n % 2
            r = slot + (slot == 2).astype(jnp.int32) - (slot == 3).astype(jnp.int32)
            rows = pl.multiple_of(pair * 16, 16)
            values = home[k, :, slot, pl.ds(rows, 16), :].reshape(PEERS * 16, LANES)
            both = lax.dot_general(
                values, table_ref[k], (((0,), (0,)), ((), ())), preferred_element_type=jnp.float32)
            lagged = (both[:, :2 * LAGS] + both[:, 2 * LAGS:]) * scale
            for c in range(2):
                piece = lagged[:, c * LAGS:(c + 1) * LAGS]
                if k == 0:
                    out_ref[r, pair * 2 + c] = piece
                else:
                    out_ref[r, pair * 2 + c] += piece
            return 0

        lax.fori_loop(0, ROUNDS * 2, body, 0)

    whiten(0)
    pl.semaphore_wait(barrier, 2 * PEERS + 6 - 2 * alone.astype(jnp.int32))
    send_in(0)
    whiten(1)
    send_in(1)
    for k in range(SUB):
        wait_in(k)
        regroup(k)
        send_ring(k)
        cross(k, 0, 0, back.at[k, 0], lambda f: pass_on(k, f))
        send_out(k, 0)
        cross(k, 0, 1, back.at[k, 1], lambda f: next_copy(k, f).wait_recv())
        for f in range(FSUB):
            third_copy(k, f).wait_recv()
        cross(k, 1, 2, loan.at[k], lambda f: None)
        loan_copy(k).start()
        cross(k, 0, 2, back.at[k, 2], lambda f: None)
        loan_copy(k).wait_recv()
        send_out(k, 1)
    for k in range(SUB):
        wait_out(k)
        to_lags(k)

    for k in range(SUB):
        end_ring(k)

        def finish(n, _):
            @pl.when(jnp.logical_not(jnp.logical_and(alone, n == chunk)))
            def _():
                in_copy(k, n, dev).wait_send()

            @pl.when(jnp.logical_not(jnp.logical_and(alone, n == dev)))
            def _():
                for late in range(2):
                    out_copy(k, late, n, chunk).wait_send()

            return 0

        lax.fori_loop(0, PEERS, finish, 0)


def local(spectra, validity):
    pieces = spectra.reshape(PARTS, PEERS, SUB, FSUB, OWN, WINDOWS).transpose(2, 1, 0, 4, 3, 5)
    pieces = pieces.reshape(SUB, PEERS, PARTS, ROWS, WINDOWS)
    mask = jnp.repeat(validity.astype(jnp.float32), FSUB, axis=0)
    table = jnp.asarray(lag_table())
    vmem = pl.BlockSpec(memory_space=pltpu.VMEM)
    dma = pltpu.SemaphoreType.DMA
    return pl.pallas_call(
        kernel,
        out_shape=jax.ShapeDtypeStruct((ROUNDS, OWN, GROUP, LAGS), jnp.float32),
        in_specs=[vmem, vmem, vmem],
        out_specs=vmem,
        scratch_shapes=[
            pltpu.VMEM((SUB, PEERS, PARTS, ROWS, WINDOWS), jnp.bfloat16),
            pltpu.VMEM((SUB, PEERS, PARTS, ROWS, WINDOWS), jnp.bfloat16),
            pltpu.VMEM((WINDOWS // LANES, PEERS * ROWS, LANES), jnp.float32),
            pltpu.VMEM((SUB, 3, FSUB, GROUP, PARTS * WINDOWS), jnp.bfloat16),
            pltpu.VMEM((SUB, FSUB, GROUP, PARTS * WINDOWS), jnp.bfloat16),
            pltpu.VMEM((2 * GROUP, PARTS * WINDOWS), jnp.bfloat16),
            pltpu.VMEM((GROUP * PARTS * FSUB, LANES), jnp.float32),
            pltpu.VMEM((SUB, PEERS, BACK_ROWS, LANES), jnp.bfloat16),
            pltpu.VMEM((SUB, ROUNDS, PEERS, BACK_ROWS, LANES), jnp.bfloat16),
            pltpu.VMEM((SUB, PEERS, ROUNDS, BACK_ROWS, LANES), jnp.bfloat16),
            dma((SUB, PEERS)), dma((SUB, PEERS)),
            dma((SUB, 4, FSUB)), dma((SUB, 4, FSUB)),
            dma((SUB, 2, PEERS)), dma((SUB, 2, PEERS)),
            dma((3 * SUB,)),
        ],
        compiler_params=pltpu.CompilerParams(
            collective_id=1, has_side_effects=True, vmem_limit_bytes=48 << 20),
        name="correlate",
    )(pieces, mask, table)


def solution(mesh):
    in_specs = (P(None, None, ("grp", "dev"), None), P(("grp", "dev"), None))
    out_specs = P(None, ("grp", "dev"), None, None)
    return jax.shard_map(local, mesh=mesh, in_specs=in_specs, out_specs=out_specs, check_vma=False)
```

```python
import jax
import jax.numpy as jnp
import numpy as np
from jax import lax
from jax.experimental import pallas as pl
from jax.experimental.pallas import tpu as pltpu
from jax.sharding import PartitionSpec as P

MESH = pl.DeviceIdType.MESH
FREQS = 256
LAGS = 128
ROUNDS = 4
WINDOWS = 384
GROUP = 128
PEERS = 32
PARTS = 2
SUB = 2
FSUB = FREQS // PEERS // SUB
OWN = GROUP // PEERS
ROWS = OWN * FSUB
BACK_ROWS = OWN * PARTS * FSUB
LANES = 128
PLANE_ROWS = 4 * PARTS * FSUB
BATCH = 4
PLANES = 16
REACH = 7
NEAR = 3
PLACES = 2 * REACH + NEAR
HOP = 2
BATCHES = (((0, 1), (1, 4)), ((0, 1), (1, 2), (2, 3), (3, 4)))


def lag_table():
    freq = np.arange(FREQS, dtype=np.int64)[:, None]
    lag = np.arange(LAGS, dtype=np.int64)[None, :] - LAGS // 2
    angle = np.pi * np.mod(freq * lag, 2 * FREQS) / FREQS
    signed = np.stack([np.cos(angle), -np.sin(angle)], axis=0).astype(np.float32)
    upper = signed.astype(jnp.bfloat16)
    lower = (signed - upper.astype(np.float32)).astype(jnp.bfloat16)
    split = np.stack([upper, lower], axis=0)
    split = split.reshape(2, PARTS, SUB, PEERS, FSUB, LAGS)
    split = split.transpose(2, 3, 1, 4, 0, 5)
    table = np.zeros((SUB, PEERS, 2, PARTS, FSUB, 2, 2, LAGS), dtype=jnp.bfloat16)
    for pair in range(2):
        table[:, :, pair, :, :, :, pair, :] = split
    table = table.reshape(SUB, PEERS * 2 * PARTS * FSUB, 4 * LAGS)
    return np.concatenate([table, table[:, :(REACH - 1) * PLANE_ROWS]], axis=1)


def kernel(x_hbm, valid_ref, table_hbm, out_ref, x_ref, table_ref, stage, send, recv, spread, blocks, carry, left, terms, loan, back, home, sums, part, got,
           send_sem, recv_sem, ring_send, ring_recv, back_send, back_recv, part_send, part_recv, self_sem, load_sem):
    grp = lax.axis_index("grp")
    dev = lax.axis_index("dev")
    z_lo, y = grp // 4, grp % 4
    x, z_hi, core = dev // 8, (dev // 2) % 4, dev % 2
    plane = z_hi * 4 + z_lo
    chunk = plane * 2 + core
    flip = 1 - 2 * (z_lo % 2)
    held = (z_lo + flip * x + 4) % 4
    alone = x == 0

    def worker(q):
        at = q // 2
        column = ((z_lo - at) * (1 - 2 * (at % 2)) + 32) % 4
        return (at % 4 * 4 + y, column * 8 + at // 4 * 2 + q % 2)

    def owner(s):
        return (held * 4 + y, s)

    def at_plane(at):
        return (at % 4 * 4 + y, x * 8 + at // 4 * 2 + core)

    def load_x(k):
        half = pl.ds(k * FREQS // SUB, FREQS // SUB)
        return pltpu.make_async_copy(x_hbm.at[:, half], x_ref.at[:, half], load_sem.at[k])

    load_table = pltpu.make_async_copy(table_hbm, table_ref, load_sem.at[SUB])
    for k in range(SUB):
        load_x(k).start()
    load_table.start()

    def route(n):
        s = (x + n // 4) % 4 * 8 + (z_hi + 2 + n) % 4 * 2 + (core + n // 16) % 2
        goal = s // 2 % 4 * 4 + held
        away = (plane - goal + 7 + PLANES) % PLANES - 7
        away = away - PLANES * jnp.logical_and(away == 8, held % 2 == 1).astype(jnp.int32)
        after, before = (away >= HOP).astype(jnp.int32), (away <= -HOP).astype(jnp.int32)
        place = away + 15 - after * 17
        stop = (goal + HOP * (after - before) + PLANES) % PLANES
        here = jnp.logical_and(stop == plane, jnp.logical_and(s // 8 == x, s % 2 == core))
        return s, place, (stop % 4 * 4 + y, s // 8 * 8 + stop // 4 * 2 + s % 2), here

    def origin(place, c):
        if place < REACH:
            goal, at = plane - HOP, plane + place
        elif place < 2 * REACH:
            goal, at = plane + HOP, plane + place - 13
        else:
            goal, at = plane, plane + place - 15
        at = (at + PLANES) % PLANES
        column = (((goal + PLANES) % 4 - at) * (1 - 2 * (at % 2)) + 32) % 4
        here = jnp.logical_and(at == plane, jnp.logical_and(column == x, c == core))
        return (at % 4 * 4 + y, column * 8 + at // 4 * 2 + c), here

    odd = z_lo % 2
    unused = lax.select(odd == 1, jnp.int32(REACH - 1), jnp.int32(REACH))

    def ring(by):
        g = (held * 4 + y + by + 16) % 16
        column = ((g // 4 - z_lo) * flip + 8) % 4
        return (z_lo * 4 + g % 4, column * 8 + z_hi * 2 + core)

    barrier = pltpu.get_barrier_semaphore()

    for i in range(PEERS):
        @pl.when(jnp.logical_not(jnp.logical_and(alone, i == dev)))
        def _():
            pl.semaphore_signal(barrier, inc=1, device_id=owner(i), device_id_type=MESH)


    for place in range(PLACES):
        for c in range(2):
            source, here = origin(place, c)
            far = jnp.logical_not(here)
            if place in (REACH - 1, REACH):
                far = jnp.logical_and(far, place != unused)

            @pl.when(far)
            def _():
                pl.semaphore_signal(barrier, inc=1, device_id=source, device_id_type=MESH)

    for by in (HOP, -HOP):
        pl.semaphore_signal(barrier, inc=1, device_id=at_plane((plane + by + PLANES) % PLANES), device_id_type=MESH)
    for by in (-1, -3, 3, -4, 1):
        pl.semaphore_signal(barrier, inc=1, device_id=ring(by), device_id_type=MESH)

    def in_copy(k, q, s):
        return pltpu.make_async_remote_copy(
            src_ref=send.at[k, q], dst_ref=recv.at[k, s], send_sem=send_sem.at[k, q],
            recv_sem=recv_sem.at[k, s], device_id=worker(q), device_id_type=MESH)

    def in_self(k):
        return pltpu.make_async_copy(send.at[k, chunk], recv.at[k, dev], self_sem.at[k])

    def nth(n):
        step = n // 2
        off = lax.select(step % 2 == 0, 8 - step // 2, step // 2 - 7)
        return (plane + off + 16) % 16 * 2 + (core + n) % 2

    def put(k, q):
        here = jnp.logical_and(alone, q == chunk)

        @pl.when(jnp.logical_not(here))
        def _():
            in_copy(k, q, dev).start()

        @pl.when(here)
        def _():
            in_self(k).start()

    def send_in(k):
        def body(n, _):
            for b in range(BATCH):
                q = nth(n * BATCH + b)
                at = (k * PEERS + q) * FSUB
                masked = x_ref[:, pl.ds(at, FSUB)].astype(jnp.float32) * valid_ref[...].astype(jnp.float32)[None, None]
                power = jnp.sum(jnp.sum(masked * masked, axis=0, keepdims=True), axis=3, keepdims=True) / WINDOWS + 1e-06
                whitened = masked / jnp.sqrt(power)
                for part in range(PARTS):
                    for w in range(WINDOWS // LANES):
                        for f in range(FSUB):
                            stage[b, part, w, pl.ds(f, OWN, stride=FSUB), :] = whitened[
                                part, f, :, w * LANES:(w + 1) * LANES]
            for b in range(BATCH):
                for part in range(PARTS):
                    for w in range(WINDOWS // LANES):
                        send[k, nth(n * BATCH + b), part, :, w * LANES:(w + 1) * LANES] = stage[b, part, w].astype(jnp.bfloat16)
            for b in range(BATCH):
                put(k, nth(n * BATCH + b))
            return 0

        lax.fori_loop(0, PEERS // BATCH, body, 0)

    def wait_in(k):
        def body(s, _):
            here = jnp.logical_and(alone, s == dev)

            @pl.when(jnp.logical_not(here))
            def _():
                in_copy(k, s, s).wait_recv()

            @pl.when(here)
            def _():
                in_self(k).wait()

            return 0

        lax.fori_loop(0, PEERS, body, 0)

    def regroup(k):
        for part in range(PARTS):
            for w in range(WINDOWS // LANES):
                spread[w] = recv[k, :, part, :, w * LANES:(w + 1) * LANES].astype(jnp.float32).reshape(
                    PEERS * ROWS, LANES)
            for f in range(FSUB):
                for w in range(WINDOWS // LANES):
                    at = part * WINDOWS + w * LANES
                    blocks[k, 0, f, :, at:at + LANES] = spread[
                        w, pl.ds(f, GROUP, stride=FSUB), :].astype(jnp.bfloat16)

    def ring_copy(by, src, dst, k, which, f):
        return pltpu.make_async_remote_copy(
            src_ref=src, dst_ref=dst, send_sem=ring_send.at[k, which, f], recv_sem=ring_recv.at[k, which, f],
            device_id=ring(by), device_id_type=MESH)

    def next_copy(k, f):
        return ring_copy(1, blocks.at[k, 0, f], blocks.at[k, 1, f], k, 0, f)

    def third_copy(k, f):
        return ring_copy(3, blocks.at[k, 0, f], blocks.at[k, 2, f], k, 1, f)

    def turn_copy(k, f):
        return ring_copy(-3, blocks.at[k, 0, f], carry.at[k, f], k, 2, f)

    def pass_copy(k, f):
        return ring_copy(4, carry.at[k, f], blocks.at[k, 1, f], k, 0, f)

    def loan_copy(k):
        return ring_copy(-1, loan.at[k], back.at[k, 3], k, 3, 0)

    def send_ring(k):
        next_copy(k, FSUB - 1).start()
        for f in range(FSUB):
            if f < FSUB - 1:
                @pl.when(y < 3)
                def _():
                    next_copy(k, f).start()

                @pl.when(y == 3)
                def _():
                    turn_copy(k, f).start()

            third_copy(k, f).start()

    def pass_on(k, f):
        @pl.when(jnp.logical_and(y == 0, f < FSUB - 1))
        def _():
            turn_copy(k, f).wait_recv()
            pass_copy(k, f).start()

    def end_ring(k):
        next_copy(k, FSUB - 1).wait_send()
        for f in range(FSUB):
            if f < FSUB - 1:
                @pl.when(y < 3)
                def _():
                    next_copy(k, f).wait_send()

                @pl.when(y == 3)
                def _():
                    turn_copy(k, f).wait_send()

                @pl.when(y == 0)
                def _():
                    pass_copy(k, f).wait_send()

            third_copy(k, f).wait_send()
        loan_copy(k).wait_send()

    def cross(k, one, other, put, ready):
        def body(f, _):
            ready(f)
            own = blocks[k, one, f]
            left[0:GROUP, :] = own
            left[GROUP:, 0:WINDOWS] = own[:, WINDOWS:]
            left[GROUP:, WINDOWS:] = -own[:, :WINDOWS]
            product = lax.dot_general(
                left[...], blocks[k, other, f], (((1,), (1,)), ((), ())), preferred_element_type=jnp.float32)
            for part in range(PARTS):
                terms[pl.ds(part * FSUB + f, GROUP, stride=PARTS * FSUB), :] = product[
                    part * GROUP:(part + 1) * GROUP]
            return 0

        lax.fori_loop(0, FSUB, body, 0)
        put[...] = terms[...].astype(jnp.bfloat16).reshape(PEERS, BACK_ROWS, LANES)

    def out_refs(k, late, s, place, c):
        first, last = BATCHES[k][late]
        return back.at[k, first:last, s], home.at[k, place, c, first:last]

    def out_copy(k, late, n):
        s, place, target, here = route(n)
        src, dst = out_refs(k, late, s, place, core)
        far = pltpu.make_async_remote_copy(
            src_ref=src, dst_ref=dst, send_sem=back_send.at[k, late, n],
            recv_sem=back_recv.at[k, late, place, core], device_id=target, device_id_type=MESH)
        return here, far, pltpu.make_async_copy(src, dst, back_recv.at[k, late, place, core])

    def send_out(k, late):
        def body(n, _):
            here, far, near = out_copy(k, late, n)

            @pl.when(jnp.logical_not(here))
            def _():
                far.start()

            @pl.when(here)
            def _():
                near.start()

            return 0

        lax.fori_loop(0, PEERS, body, 0)

    def wait_out(k, late, lowest, highest):
        def body(n, _):
            place, c = n // 2, n % 2

            @pl.when(place != unused)
            def _():
                _, dst = out_refs(k, late, 0, place, c)
                pltpu.make_async_copy(dst, dst, back_recv.at[k, late, place, c]).wait()

            return 0

        lax.fori_loop(2 * lowest, 2 * highest, body, 0)

    scale = 1.0 / np.sqrt(np.float32(WINDOWS) * FREQS)

    def lags(k, lowest, count, start, slot, pair):
        rows = pl.multiple_of(pair * 16, 16)
        values = home[k, lowest:lowest + count, :, slot, pl.ds(rows, 16), :].reshape(count * PLANE_ROWS, LANES)
        window = pl.ds(pl.multiple_of((start + PLANES) % PLANES * PLANE_ROWS, PLANE_ROWS), count * PLANE_ROWS)
        both = lax.dot_general(
            values, table_ref[k, window, :], (((0,), (0,)), ((), ())), preferred_element_type=jnp.float32)
        return (both[:, :2 * LAGS] + both[:, 2 * LAGS:]) * scale

    def reach_lags(k, side, slot, pair):
        return lags(k, side * REACH, REACH, plane - side * (REACH - 1), slot, pair)

    def gather_first():
        def body(n, _):
            slot, pair = n // 2, n % 2
            for side in range(2):
                values = reach_lags(0, side, slot, pair)
                for c in range(2):
                    sums[side, slot, pair * 2 + c] = values[:, c * LAGS:(c + 1) * LAGS]
            return 0

        lax.fori_loop(0, ROUNDS * 2, body, 0)

    def part_copy(side, slot):
        goal = (plane + (2 * side - 1) * HOP + PLANES) % PLANES
        return pltpu.make_async_remote_copy(
            src_ref=part.at[side, slot], dst_ref=got.at[side, slot], send_sem=part_send.at[side, slot],
            recv_sem=part_recv.at[side, slot], device_id=at_plane(goal), device_id_type=MESH)

    def gather_last(slot):
        def body(pair, _):
            for side in range(2):
                values = reach_lags(1, side, slot, pair)
                for c in range(2):
                    total = sums[side, slot, pair * 2 + c] + values[:, c * LAGS:(c + 1) * LAGS]
                    part[side, slot, pair * 2 + c] = total.astype(jnp.bfloat16)
            return 0

        lax.fori_loop(0, 2, body, 0)
        for side in range(2):
            part_copy(side, slot).start()

    def round_of(slot):
        return slot + (slot == 2).astype(jnp.int32) - (slot == 3).astype(jnp.int32)

    def near_lags():
        def body(n, _):
            slot, pair = n // 2, n % 2
            values = lags(0, 2 * REACH, NEAR, plane - 1, slot, pair) + lags(1, 2 * REACH, NEAR, plane - 1, slot, pair)
            for c in range(2):
                out_ref[round_of(slot), pair * 2 + c] = values[:, c * LAGS:(c + 1) * LAGS]
            return 0

        lax.fori_loop(0, ROUNDS * 2, body, 0)

    def add_parts(slot):
        def body(c, _):
            r = (0, 1, 3, 2)[slot]
            out_ref[r, c] += got[0, slot, c].astype(jnp.float32) + got[1, slot, c].astype(jnp.float32)
            return 0

        lax.fori_loop(0, OWN, body, 0)

    for k in range(SUB):
        home[k, unused] = jnp.zeros((2, ROUNDS, BACK_ROWS, LANES), jnp.bfloat16)
    load_x(0).wait()
    targets = 2 * PEERS + 7 - 2 * (x == 0).astype(jnp.int32) - 2 * (x == 2).astype(jnp.int32)
    pl.semaphore_wait(barrier, targets)
    send_in(0)
    load_x(1).wait()
    send_in(1)
    for k in range(SUB):
        wait_in(k)
        regroup(k)
        send_ring(k)
        cross(k, 0, 0, back.at[k, 0], lambda f: pass_on(k, f))
        send_out(k, 0)
        cross(k, 0, 1, back.at[k, 1], lambda f: next_copy(k, f).wait_recv())
        if k > 0:
            send_out(k, 1)
        for f in range(FSUB):
            third_copy(k, f).wait_recv()
        cross(k, 1, 2, loan.at[k], lambda f: None)
        loan_copy(k).start()
        cross(k, 0, 2, back.at[k, 2], lambda f: None)
        if k > 0:
            send_out(k, 2)
        loan_copy(k).wait_recv()
        send_out(k, len(BATCHES[k]) - 1)
    load_table.wait()
    wait_out(0, 0, 0, 2 * REACH)
    wait_out(0, 1, 0, 2 * REACH)
    gather_first()
    for slot in range(ROUNDS):
        wait_out(1, slot, 0, 2 * REACH)
        gather_last(slot)
    for k in range(SUB):
        for late in range(len(BATCHES[k])):
            wait_out(k, late, 2 * REACH, PLACES)
    near_lags()
    for slot in range(ROUNDS):
        for side in range(2):
            part_copy(side, slot).wait_recv()
        add_parts(slot)
    for slot in range(ROUNDS):
        for side in range(2):
            part_copy(side, slot).wait_send()
    for k in range(SUB):
        end_ring(k)

        def finish(n, _):
            @pl.when(jnp.logical_not(jnp.logical_and(alone, n == chunk)))
            def _():
                in_copy(k, n, dev).wait_send()

            for late in range(len(BATCHES[k])):
                here, far, _ = out_copy(k, late, n)

                @pl.when(jnp.logical_not(here))
                def _():
                    far.wait_send()

            return 0

        lax.fori_loop(0, PEERS, finish, 0)


def local(spectra, validity):
    table = jnp.asarray(lag_table())
    vmem = pl.BlockSpec(memory_space=pltpu.VMEM)
    anywhere = pl.BlockSpec(memory_space=pl.ANY)
    dma = pltpu.SemaphoreType.DMA
    return pl.pallas_call(
        kernel,
        out_shape=jax.ShapeDtypeStruct((ROUNDS, OWN, GROUP, LAGS), jnp.float32),
        in_specs=[anywhere, vmem, anywhere],
        out_specs=vmem,
        scratch_shapes=[
            pltpu.VMEM((PARTS, FREQS, OWN, WINDOWS), jnp.bfloat16),
            pltpu.VMEM((SUB, (PLANES + REACH - 1) * PLANE_ROWS, 4 * LANES), jnp.bfloat16),
            pltpu.VMEM((BATCH, PARTS, WINDOWS // LANES, ROWS, LANES), jnp.float32),
            pltpu.VMEM((SUB, PEERS, PARTS, ROWS, WINDOWS), jnp.bfloat16),
            pltpu.VMEM((SUB, PEERS, PARTS, ROWS, WINDOWS), jnp.bfloat16),
            pltpu.VMEM((WINDOWS // LANES, PEERS * ROWS, LANES), jnp.float32),
            pltpu.VMEM((SUB, 3, FSUB, GROUP, PARTS * WINDOWS), jnp.bfloat16),
            pltpu.VMEM((SUB, FSUB, GROUP, PARTS * WINDOWS), jnp.bfloat16),
            pltpu.VMEM((2 * GROUP, PARTS * WINDOWS), jnp.bfloat16),
            pltpu.VMEM((GROUP * PARTS * FSUB, LANES), jnp.float32),
            pltpu.VMEM((SUB, PEERS, BACK_ROWS, LANES), jnp.bfloat16),
            pltpu.VMEM((SUB, ROUNDS, PEERS, BACK_ROWS, LANES), jnp.bfloat16),
            pltpu.VMEM((SUB, PLACES, 2, ROUNDS, BACK_ROWS, LANES), jnp.bfloat16),
            pltpu.VMEM((2, ROUNDS, OWN, GROUP, LAGS), jnp.float32),
            pltpu.VMEM((2, ROUNDS, OWN, GROUP, LAGS), jnp.bfloat16),
            pltpu.VMEM((2, ROUNDS, OWN, GROUP, LAGS), jnp.bfloat16),
            dma((SUB, PEERS)), dma((SUB, PEERS)),
            dma((SUB, 4, FSUB)), dma((SUB, 4, FSUB)),
            dma((SUB, ROUNDS, PEERS)), dma((SUB, ROUNDS, PLACES, 2)),
            dma((2, ROUNDS)), dma((2, ROUNDS)),
            dma((SUB,)), dma((SUB + 1,)),
        ],
        compiler_params=pltpu.CompilerParams(
            collective_id=1, has_side_effects=True, vmem_limit_bytes=56 << 20),
        name="correlate",
    )(spectra, validity, table)


def solution(mesh):
    in_specs = (P(None, None, ("grp", "dev"), None), P(("grp", "dev"), None))
    out_specs = P(None, ("grp", "dev"), None, None)
    return jax.shard_map(local, mesh=mesh, in_specs=in_specs, out_specs=out_specs, check_vma=False)
```

```python
import jax
import jax.numpy as jnp
import numpy as np
from jax import lax
from jax.experimental import pallas as pl
from jax.experimental.pallas import tpu as pltpu
from jax.sharding import PartitionSpec as P

MESH = pl.DeviceIdType.MESH
FREQS = 256
LAGS = 128
ROUNDS = 4
WINDOWS = 384
GROUP = 128
PEERS = 32
PARTS = 2
SUB = 2
FSUB = FREQS // PEERS // SUB
OWN = GROUP // PEERS
ROWS = OWN * FSUB
BACK_ROWS = OWN * PARTS * FSUB
LANES = 128
PLANE_ROWS = 4 * PARTS * FSUB
BATCH = 4
PLANES = 16
REACH = 7
NEAR = 3
PLACES = 2 * REACH + NEAR
HOP = 2
BATCHES = (((0, 1), (1, 4)), ((0, 1), (1, 2), (2, 3), (3, 4)))


def lag_table():
    freq = np.arange(FREQS, dtype=np.int64)[:, None]
    lag = np.arange(LAGS, dtype=np.int64)[None, :] - LAGS // 2
    angle = np.pi * np.mod(freq * lag, 2 * FREQS) / FREQS
    signed = np.stack([np.cos(angle), -np.sin(angle)], axis=0).astype(np.float32)
    upper = signed.astype(jnp.bfloat16)
    lower = (signed - upper.astype(np.float32)).astype(jnp.bfloat16)
    split = np.stack([upper, lower], axis=0)
    split = split.reshape(2, PARTS, SUB, PEERS, FSUB, LAGS)
    split = split.transpose(2, 3, 1, 4, 0, 5)
    table = np.zeros((SUB, PEERS, 2, PARTS, FSUB, 2, 2, LAGS), dtype=jnp.bfloat16)
    for pair in range(2):
        table[:, :, pair, :, :, :, pair, :] = split
    table = table.reshape(SUB, PEERS * 2 * PARTS * FSUB, 4 * LAGS)
    return np.concatenate([table, table[:, :(REACH - 1) * PLANE_ROWS]], axis=1)


def kernel(x_hbm, valid_ref, table_hbm, out_ref, x_ref, table_ref, stage, send, recv, spread, blocks, carry, left, terms, loan, back, home, sums, part, got,
           send_sem, recv_sem, ring_send, ring_recv, back_send, back_recv, part_send, part_recv, self_sem, load_sem):
    grp = lax.axis_index("grp")
    dev = lax.axis_index("dev")
    z_lo, y = grp // 4, grp % 4
    x, z_hi, core = dev // 8, (dev // 2) % 4, dev % 2
    plane = z_hi * 4 + z_lo
    chunk = plane * 2 + core
    flip = 1 - 2 * (z_lo % 2)
    held = (z_lo + flip * x + 4) % 4
    alone = x == 0

    def worker(q):
        at = q // 2
        column = ((z_lo - at) * (1 - 2 * (at % 2)) + 32) % 4
        return (at % 4 * 4 + y, column * 8 + at // 4 * 2 + q % 2)

    def owner(s):
        return (held * 4 + y, s)

    def at_plane(at):
        return (at % 4 * 4 + y, x * 8 + at // 4 * 2 + core)

    def load_x(k):
        half = pl.ds(k * FREQS // SUB, FREQS // SUB)
        return pltpu.make_async_copy(x_hbm.at[:, half], x_ref.at[:, half], load_sem.at[k])

    load_table = pltpu.make_async_copy(table_hbm, table_ref, load_sem.at[SUB])
    for k in range(SUB):
        load_x(k).start()
    load_table.start()

    def route(n):
        s = (x + n // 4) % 4 * 8 + (z_hi + 2 + n) % 4 * 2 + (core + n // 16) % 2
        goal = s // 2 % 4 * 4 + held
        away = (plane - goal + 7 + PLANES) % PLANES - 7
        away = away - PLANES * jnp.logical_and(away == 8, held % 2 == 1).astype(jnp.int32)
        after, before = (away >= HOP).astype(jnp.int32), (away <= -HOP).astype(jnp.int32)
        place = away + 15 - after * 17
        stop = (goal + HOP * (after - before) + PLANES) % PLANES
        here = jnp.logical_and(stop == plane, jnp.logical_and(s // 8 == x, s % 2 == core))
        return s, place, (stop % 4 * 4 + y, s // 8 * 8 + stop // 4 * 2 + s % 2), here

    def origin(place, c):
        if place < REACH:
            goal, at = plane - HOP, plane + place
        elif place < 2 * REACH:
            goal, at = plane + HOP, plane + place - 13
        else:
            goal, at = plane, plane + place - 15
        at = (at + PLANES) % PLANES
        column = (((goal + PLANES) % 4 - at) * (1 - 2 * (at % 2)) + 32) % 4
        here = jnp.logical_and(at == plane, jnp.logical_and(column == x, c == core))
        return (at % 4 * 4 + y, column * 8 + at // 4 * 2 + c), here

    odd = z_lo % 2
    unused = lax.select(odd == 1, jnp.int32(REACH - 1), jnp.int32(REACH))

    def ring(by):
        g = (held * 4 + y + by + 16) % 16
        column = ((g // 4 - z_lo) * flip + 8) % 4
        return (z_lo * 4 + g % 4, column * 8 + z_hi * 2 + core)

    barrier = pltpu.get_barrier_semaphore()

    for i in range(PEERS):
        @pl.when(jnp.logical_not(jnp.logical_and(alone, i == dev)))
        def _():
            pl.semaphore_signal(barrier, inc=1, device_id=owner(i), device_id_type=MESH)


    for place in range(PLACES):
        for c in range(2):
            source, here = origin(place, c)
            far = jnp.logical_not(here)
            if place in (REACH - 1, REACH):
                far = jnp.logical_and(far, place != unused)

            @pl.when(far)
            def _():
                pl.semaphore_signal(barrier, inc=1, device_id=source, device_id_type=MESH)

    for by in (HOP, -HOP):
        pl.semaphore_signal(barrier, inc=1, device_id=at_plane((plane + by + PLANES) % PLANES), device_id_type=MESH)
    for by in (-1, -3, 3, -4, 1):
        pl.semaphore_signal(barrier, inc=1, device_id=ring(by), device_id_type=MESH)

    def in_copy(k, q, s):
        return pltpu.make_async_remote_copy(
            src_ref=send.at[k, q], dst_ref=recv.at[k, s], send_sem=send_sem.at[k, q],
            recv_sem=recv_sem.at[k, s], device_id=worker(q), device_id_type=MESH)

    def in_self(k):
        return pltpu.make_async_copy(send.at[k, chunk], recv.at[k, dev], self_sem.at[k])

    def nth(n):
        step = n // 2
        off = lax.select(step % 2 == 0, 8 - step // 2, step // 2 - 7)
        return (plane + off + 16) % 16 * 2 + (core + n) % 2

    def put(k, q):
        here = jnp.logical_and(alone, q == chunk)

        @pl.when(jnp.logical_not(here))
        def _():
            in_copy(k, q, dev).start()

        @pl.when(here)
        def _():
            in_self(k).start()

    def send_in(k):
        def body(n, _):
            for b in range(BATCH):
                q = nth(n * BATCH + b)
                at = (k * PEERS + q) * FSUB
                masked = x_ref[:, pl.ds(at, FSUB)].astype(jnp.float32) * valid_ref[...].astype(jnp.float32)[None, None]
                power = jnp.sum(jnp.sum(masked * masked, axis=0, keepdims=True), axis=3, keepdims=True) / WINDOWS + 1e-06
                whitened = masked / jnp.sqrt(power)
                for part in range(PARTS):
                    for w in range(WINDOWS // LANES):
                        for f in range(FSUB):
                            stage[b, part, w, pl.ds(f, OWN, stride=FSUB), :] = whitened[
                                part, f, :, w * LANES:(w + 1) * LANES]
            for b in range(BATCH):
                for part in range(PARTS):
                    for w in range(WINDOWS // LANES):
                        send[k, nth(n * BATCH + b), part, :, w * LANES:(w + 1) * LANES] = stage[b, part, w].astype(jnp.bfloat16)
            for b in range(BATCH):
                put(k, nth(n * BATCH + b))
            return 0

        lax.fori_loop(0, PEERS // BATCH, body, 0)

    def wait_in(k):
        def body(s, _):
            here = jnp.logical_and(alone, s == dev)

            @pl.when(jnp.logical_not(here))
            def _():
                in_copy(k, s, s).wait_recv()

            @pl.when(here)
            def _():
                in_self(k).wait()

            return 0

        lax.fori_loop(0, PEERS, body, 0)

    def regroup(k):
        for part in range(PARTS):
            for w in range(WINDOWS // LANES):
                spread[w] = recv[k, :, part, :, w * LANES:(w + 1) * LANES].astype(jnp.float32).reshape(
                    PEERS * ROWS, LANES)
            for f in range(FSUB):
                for w in range(WINDOWS // LANES):
                    at = part * WINDOWS + w * LANES
                    blocks[k, 0, f, :, at:at + LANES] = spread[
                        w, pl.ds(f, GROUP, stride=FSUB), :].astype(jnp.bfloat16)

    def ring_copy(by, src, dst, k, which, f):
        return pltpu.make_async_remote_copy(
            src_ref=src, dst_ref=dst, send_sem=ring_send.at[k, which, f], recv_sem=ring_recv.at[k, which, f],
            device_id=ring(by), device_id_type=MESH)

    def next_copy(k, f):
        return ring_copy(1, blocks.at[k, 0, f], blocks.at[k, 1, f], k, 0, f)

    def third_copy(k, f):
        return ring_copy(3, blocks.at[k, 0, f], blocks.at[k, 2, f], k, 1, f)

    def turn_copy(k, f):
        return ring_copy(-3, blocks.at[k, 0, f], carry.at[k, f], k, 2, f)

    def pass_copy(k, f):
        return ring_copy(4, carry.at[k, f], blocks.at[k, 1, f], k, 0, f)

    def loan_copy(k):
        return ring_copy(-1, loan.at[k], back.at[k, 3], k, 3, 0)

    def send_ring(k):
        next_copy(k, FSUB - 1).start()
        for f in range(FSUB):
            if f < FSUB - 1:
                @pl.when(y < 3)
                def _():
                    next_copy(k, f).start()

                @pl.when(y == 3)
                def _():
                    turn_copy(k, f).start()

            third_copy(k, f).start()

    def pass_on(k, f):
        @pl.when(jnp.logical_and(y == 0, f < FSUB - 1))
        def _():
            turn_copy(k, f).wait_recv()
            pass_copy(k, f).start()

    def end_ring(k):
        next_copy(k, FSUB - 1).wait_send()
        for f in range(FSUB):
            if f < FSUB - 1:
                @pl.when(y < 3)
                def _():
                    next_copy(k, f).wait_send()

                @pl.when(y == 3)
                def _():
                    turn_copy(k, f).wait_send()

                @pl.when(y == 0)
                def _():
                    pass_copy(k, f).wait_send()

            third_copy(k, f).wait_send()
        loan_copy(k).wait_send()

    def cross(k, one, other, put, ready):
        def body(f, _):
            ready(f)
            own = blocks[k, one, f]
            left[0:GROUP, :] = own
            left[GROUP:, 0:WINDOWS] = own[:, WINDOWS:]
            left[GROUP:, WINDOWS:] = -own[:, :WINDOWS]
            product = lax.dot_general(
                left[...], blocks[k, other, f], (((1,), (1,)), ((), ())), preferred_element_type=jnp.float32)
            for part in range(PARTS):
                terms[pl.ds(part * FSUB + f, GROUP, stride=PARTS * FSUB), :] = product[
                    part * GROUP:(part + 1) * GROUP]
            return 0

        lax.fori_loop(0, FSUB, body, 0)
        put[...] = terms[...].astype(jnp.bfloat16).reshape(PEERS, BACK_ROWS, LANES)

    def out_refs(k, late, s, place, c):
        first, last = BATCHES[k][late]
        return back.at[k, first:last, s], home.at[k, place, c, first:last]

    def out_copy(k, late, n):
        s, place, target, here = route(n)
        src, dst = out_refs(k, late, s, place, core)
        far = pltpu.make_async_remote_copy(
            src_ref=src, dst_ref=dst, send_sem=back_send.at[k, late, n],
            recv_sem=back_recv.at[k, late, place, core], device_id=target, device_id_type=MESH)
        return here, far, pltpu.make_async_copy(src, dst, back_recv.at[k, late, place, core])

    def send_out(k, late):
        def body(n, _):
            here, far, near = out_copy(k, late, n)

            @pl.when(jnp.logical_not(here))
            def _():
                far.start()

            @pl.when(here)
            def _():
                near.start()

            return 0

        lax.fori_loop(0, PEERS, body, 0)

    def wait_out(k, late, lowest, highest):
        def body(n, _):
            place, c = n // 2, n % 2

            @pl.when(place != unused)
            def _():
                _, dst = out_refs(k, late, 0, place, c)
                pltpu.make_async_copy(dst, dst, back_recv.at[k, late, place, c]).wait()

            return 0

        lax.fori_loop(2 * lowest, 2 * highest, body, 0)

    scale = 1.0 / np.sqrt(np.float32(WINDOWS) * FREQS)

    def lags(k, lowest, count, start, slot, pair):
        rows = pl.multiple_of(pair * 16, 16)
        values = home[k, lowest:lowest + count, :, slot, pl.ds(rows, 16), :].reshape(count * PLANE_ROWS, LANES)
        window = pl.ds(pl.multiple_of((start + PLANES) % PLANES * PLANE_ROWS, PLANE_ROWS), count * PLANE_ROWS)
        both = lax.dot_general(
            values, table_ref[k, window, :], (((0,), (0,)), ((), ())), preferred_element_type=jnp.float32)
        return (both[:, :2 * LAGS] + both[:, 2 * LAGS:]) * scale

    def reach_lags(k, side, slot, pair):
        return lags(k, side * REACH, REACH, plane - side * (REACH - 1), slot, pair)

    def gather_first():
        def body(n, _):
            slot, pair = n // 2, n % 2
            for side in range(2):
                values = reach_lags(0, side, slot, pair)
                for c in range(2):
                    sums[side, slot, pair * 2 + c] = values[:, c * LAGS:(c + 1) * LAGS]
            return 0

        lax.fori_loop(0, ROUNDS * 2, body, 0)

    def part_copy(side, slot):
        goal = (plane + (2 * side - 1) * HOP + PLANES) % PLANES
        return pltpu.make_async_remote_copy(
            src_ref=part.at[side, slot], dst_ref=got.at[side, slot], send_sem=part_send.at[side, slot],
            recv_sem=part_recv.at[side, slot], device_id=at_plane(goal), device_id_type=MESH)

    def gather_last(slot):
        def body(pair, _):
            for side in range(2):
                values = reach_lags(1, side, slot, pair)
                for c in range(2):
                    total = sums[side, slot, pair * 2 + c] + values[:, c * LAGS:(c + 1) * LAGS]
                    part[side, slot, pair * 2 + c] = total.astype(jnp.bfloat16)
            return 0

        lax.fori_loop(0, 2, body, 0)
        for side in range(2):
            part_copy(side, slot).start()

    def round_of(slot):
        return (0, 1, 3, 2)[slot]

    def near_lags(slot):
        def body(pair, _):
            values = lags(0, 2 * REACH, NEAR, plane - 1, slot, pair) + lags(1, 2 * REACH, NEAR, plane - 1, slot, pair)
            for c in range(2):
                out_ref[round_of(slot), pair * 2 + c] = values[:, c * LAGS:(c + 1) * LAGS]
            return 0

        lax.fori_loop(0, 2, body, 0)

    def add_parts(slot):
        def body(c, _):
            out_ref[round_of(slot), c] += got[0, slot, c].astype(jnp.float32) + got[1, slot, c].astype(jnp.float32)
            return 0

        lax.fori_loop(0, OWN, body, 0)

    def end_in(k):
        def body(n, _):
            @pl.when(jnp.logical_not(jnp.logical_and(alone, n == chunk)))
            def _():
                in_copy(k, n, dev).wait_send()

            return 0

        lax.fori_loop(0, PEERS, body, 0)

    def end_out(k, late):
        def body(n, _):
            here, far, _ = out_copy(k, late, n)

            @pl.when(jnp.logical_not(here))
            def _():
                far.wait_send()

            return 0

        lax.fori_loop(0, PEERS, body, 0)

    load_x(0).wait()
    targets = 2 * PEERS + 7 - 2 * (x == 0).astype(jnp.int32) - 2 * (x == 2).astype(jnp.int32)
    pl.semaphore_wait(barrier, targets)
    send_in(0)
    load_x(1).wait()
    send_in(1)
    for k in range(SUB):
        wait_in(k)
        regroup(k)
        send_ring(k)
        cross(k, 0, 0, back.at[k, 0], lambda f: pass_on(k, f))
        send_out(k, 0)
        end_in(k)
        cross(k, 0, 1, back.at[k, 1], lambda f: next_copy(k, f).wait_recv())
        if k > 0:
            send_out(k, 1)
        for f in range(FSUB):
            third_copy(k, f).wait_recv()
        cross(k, 1, 2, loan.at[k], lambda f: None)
        loan_copy(k).start()
        cross(k, 0, 2, back.at[k, 2], lambda f: None)
        if k > 0:
            send_out(k, 2)
        loan_copy(k).wait_recv()
        send_out(k, len(BATCHES[k]) - 1)
    load_table.wait()
    for k in range(SUB):
        home[k, unused] = jnp.zeros((2, ROUNDS, BACK_ROWS, LANES), jnp.bfloat16)
    wait_out(0, 0, 0, 2 * REACH)
    wait_out(0, 1, 0, 2 * REACH)
    gather_first()
    for late in range(len(BATCHES[0])):
        wait_out(0, late, 2 * REACH, PLACES)
        end_out(0, late)
    end_ring(0)
    for slot in range(ROUNDS):
        wait_out(1, slot, 0, 2 * REACH)
        gather_last(slot)
        wait_out(1, slot, 2 * REACH, PLACES)
        near_lags(slot)
        end_out(1, slot)
    end_ring(1)
    for slot in range(ROUNDS):
        for side in range(2):
            part_copy(side, slot).wait_recv()
        add_parts(slot)
    for slot in range(ROUNDS):
        for side in range(2):
            part_copy(side, slot).wait_send()


def local(spectra, validity):
    table = jnp.asarray(lag_table())
    vmem = pl.BlockSpec(memory_space=pltpu.VMEM)
    main = pl.BlockSpec(memory_space=pltpu.HBM)
    dma = pltpu.SemaphoreType.DMA
    return pl.pallas_call(
        kernel,
        out_shape=jax.ShapeDtypeStruct((ROUNDS, OWN, GROUP, LAGS), jnp.float32),
        in_specs=[main, vmem, main],
        out_specs=vmem,
        scratch_shapes=[
            pltpu.VMEM((PARTS, FREQS, OWN, WINDOWS), jnp.bfloat16),
            pltpu.VMEM((SUB, (PLANES + REACH - 1) * PLANE_ROWS, 4 * LANES), jnp.bfloat16),
            pltpu.VMEM((BATCH, PARTS, WINDOWS // LANES, ROWS, LANES), jnp.float32),
            pltpu.VMEM((SUB, PEERS, PARTS, ROWS, WINDOWS), jnp.bfloat16),
            pltpu.VMEM((SUB, PEERS, PARTS, ROWS, WINDOWS), jnp.bfloat16),
            pltpu.VMEM((WINDOWS // LANES, PEERS * ROWS, LANES), jnp.float32),
            pltpu.VMEM((SUB, 3, FSUB, GROUP, PARTS * WINDOWS), jnp.bfloat16),
            pltpu.VMEM((SUB, FSUB, GROUP, PARTS * WINDOWS), jnp.bfloat16),
            pltpu.VMEM((2 * GROUP, PARTS * WINDOWS), jnp.bfloat16),
            pltpu.VMEM((GROUP * PARTS * FSUB, LANES), jnp.float32),
            pltpu.VMEM((SUB, PEERS, BACK_ROWS, LANES), jnp.bfloat16),
            pltpu.VMEM((SUB, ROUNDS, PEERS, BACK_ROWS, LANES), jnp.bfloat16),
            pltpu.VMEM((SUB, PLACES, 2, ROUNDS, BACK_ROWS, LANES), jnp.bfloat16),
            pltpu.VMEM((2, ROUNDS, OWN, GROUP, LAGS), jnp.float32),
            pltpu.VMEM((2, ROUNDS, OWN, GROUP, LAGS), jnp.bfloat16),
            pltpu.VMEM((2, ROUNDS, OWN, GROUP, LAGS), jnp.bfloat16),
            dma((SUB, PEERS)), dma((SUB, PEERS)),
            dma((SUB, 4, FSUB)), dma((SUB, 4, FSUB)),
            dma((SUB, ROUNDS, PEERS)), dma((SUB, ROUNDS, PLACES, 2)),
            dma((2, ROUNDS)), dma((2, ROUNDS)),
            dma((SUB,)), dma((SUB + 1,)),
        ],
        compiler_params=pltpu.CompilerParams(
            collective_id=1, has_side_effects=True, vmem_limit_bytes=54 << 20),
        name="correlate",
    )(spectra, validity, table)


def solution(mesh):
    in_specs = (P(None, None, ("grp", "dev"), None), P(("grp", "dev"), None))
    out_specs = P(None, ("grp", "dev"), None, None)
    return jax.shard_map(local, mesh=mesh, in_specs=in_specs, out_specs=out_specs, check_vma=False)
```

```python
import jax
import jax.numpy as jnp
import numpy as np
from jax import lax
from jax.experimental import pallas as pl
from jax.experimental.pallas import tpu as pltpu
from jax.sharding import PartitionSpec as P

MESH = pl.DeviceIdType.MESH
FREQS = 256
LAGS = 128
ROUNDS = 4
WINDOWS = 384
GROUP = 128
PEERS = 32
PARTS = 2
SUB = 2
FSUB = FREQS // PEERS // SUB
OWN = GROUP // PEERS
ROWS = OWN * FSUB
BACK_ROWS = OWN * PARTS * FSUB
LANES = 128
PLANE_ROWS = 4 * PARTS * FSUB
BATCH = 4
PLANES = 16
REACH = 7
NEAR = 3
PLACES = 2 * REACH + NEAR
HOP = 2
BATCHES = (((0, 4),), ((0, 1), (1, 2), (2, 3), (3, 4)))


def lag_table():
    freq = np.arange(FREQS, dtype=np.int64)[:, None]
    lag = np.arange(LAGS, dtype=np.int64)[None, :] - LAGS // 2
    angle = np.pi * np.mod(freq * lag, 2 * FREQS) / FREQS
    signed = np.stack([np.cos(angle), -np.sin(angle)], axis=0).astype(np.float32)
    upper = signed.astype(jnp.bfloat16)
    lower = (signed - upper.astype(np.float32)).astype(jnp.bfloat16)
    split = np.stack([upper, lower], axis=0)
    split = split.reshape(2, PARTS, SUB, PEERS, FSUB, LAGS)
    split = split.transpose(2, 3, 1, 4, 0, 5)
    table = np.zeros((SUB, PEERS, 2, PARTS, FSUB, 2, 2, LAGS), dtype=jnp.bfloat16)
    for pair in range(2):
        table[:, :, pair, :, :, :, pair, :] = split
    table = table.reshape(SUB, PEERS * 2 * PARTS * FSUB, 4 * LAGS)
    return np.concatenate([table, table[:, :(REACH - 1) * PLANE_ROWS]], axis=1)


def kernel(x_hbm, valid_ref, table_hbm, out_ref, x_ref, table_ref, stage, send, recv, spread, blocks, carry, left, terms, loan, back, home, sums, part, got,
           send_sem, recv_sem, ring_send, ring_recv, back_send, back_recv, part_send, part_recv, self_sem, load_sem):
    grp = lax.axis_index("grp")
    dev = lax.axis_index("dev")
    z_lo, y = grp // 4, grp % 4
    x, z_hi, core = dev // 8, (dev // 2) % 4, dev % 2
    plane = z_hi * 4 + z_lo
    chunk = plane * 2 + core
    flip = 1 - 2 * (z_lo % 2)
    held = (z_lo + flip * x + 4) % 4
    alone = x == 0

    def worker(q):
        at = q // 2
        column = ((z_lo - at) * (1 - 2 * (at % 2)) + 32) % 4
        return (at % 4 * 4 + y, column * 8 + at // 4 * 2 + q % 2)

    def owner(s):
        return (held * 4 + y, s)

    def at_plane(at):
        return (at % 4 * 4 + y, x * 8 + at // 4 * 2 + core)

    def load_x(k):
        half = pl.ds(k * FREQS // SUB, FREQS // SUB)
        return pltpu.make_async_copy(x_hbm.at[:, half], x_ref.at[:, half], load_sem.at[k])

    load_table = pltpu.make_async_copy(table_hbm, table_ref, load_sem.at[SUB])
    for k in range(SUB):
        load_x(k).start()
    load_table.start()

    def route(n):
        s = (x + n // 4) % 4 * 8 + (z_hi + 2 + n) % 4 * 2 + (core + n // 16) % 2
        goal = s // 2 % 4 * 4 + held
        away = (plane - goal + 7 + PLANES) % PLANES - 7
        away = away - PLANES * jnp.logical_and(away == 8, held % 2 == 1).astype(jnp.int32)
        after, before = (away >= HOP).astype(jnp.int32), (away <= -HOP).astype(jnp.int32)
        place = away + 15 - after * 17
        stop = (goal + HOP * (after - before) + PLANES) % PLANES
        here = jnp.logical_and(stop == plane, jnp.logical_and(s // 8 == x, s % 2 == core))
        return s, place, (stop % 4 * 4 + y, s // 8 * 8 + stop // 4 * 2 + s % 2), here

    def origin(place, c):
        if place < REACH:
            goal, at = plane - HOP, plane + place
        elif place < 2 * REACH:
            goal, at = plane + HOP, plane + place - 13
        else:
            goal, at = plane, plane + place - 15
        at = (at + PLANES) % PLANES
        column = (((goal + PLANES) % 4 - at) * (1 - 2 * (at % 2)) + 32) % 4
        here = jnp.logical_and(at == plane, jnp.logical_and(column == x, c == core))
        return (at % 4 * 4 + y, column * 8 + at // 4 * 2 + c), here

    odd = z_lo % 2
    unused = lax.select(odd == 1, jnp.int32(REACH - 1), jnp.int32(REACH))

    def ring(by):
        g = (held * 4 + y + by + 16) % 16
        column = ((g // 4 - z_lo) * flip + 8) % 4
        return (z_lo * 4 + g % 4, column * 8 + z_hi * 2 + core)

    barrier = pltpu.get_barrier_semaphore()

    for i in range(PEERS):
        @pl.when(jnp.logical_not(jnp.logical_and(alone, i == dev)))
        def _():
            pl.semaphore_signal(barrier, inc=1, device_id=owner(i), device_id_type=MESH)


    for place in range(PLACES):
        for c in range(2):
            source, here = origin(place, c)
            far = jnp.logical_not(here)
            if place in (REACH - 1, REACH):
                far = jnp.logical_and(far, place != unused)

            @pl.when(far)
            def _():
                pl.semaphore_signal(barrier, inc=1, device_id=source, device_id_type=MESH)

    for by in (HOP, -HOP):
        pl.semaphore_signal(barrier, inc=1, device_id=at_plane((plane + by + PLANES) % PLANES), device_id_type=MESH)
    for by in (-1, -3, 3, -4, 1):
        pl.semaphore_signal(barrier, inc=1, device_id=ring(by), device_id_type=MESH)

    def in_copy(k, q, s):
        return pltpu.make_async_remote_copy(
            src_ref=send.at[k, q], dst_ref=recv.at[k, s], send_sem=send_sem.at[k, q],
            recv_sem=recv_sem.at[k, s], device_id=worker(q), device_id_type=MESH)

    def in_self(k):
        return pltpu.make_async_copy(send.at[k, chunk], recv.at[k, dev], self_sem.at[k])

    def nth(n):
        step = n // 2
        off = lax.select(step % 2 == 0, 8 - step // 2, step // 2 - 7)
        return (plane + off + 16) % 16 * 2 + (core + n) % 2

    def put(k, q):
        here = jnp.logical_and(alone, q == chunk)

        @pl.when(jnp.logical_not(here))
        def _():
            in_copy(k, q, dev).start()

        @pl.when(here)
        def _():
            in_self(k).start()

    def send_in(k):
        def body(n, _):
            for b in range(BATCH):
                q = nth(n * BATCH + b)
                at = (k * PEERS + q) * FSUB
                masked = x_ref[:, pl.ds(at, FSUB)].astype(jnp.float32) * valid_ref[...].astype(jnp.float32)[None, None]
                power = jnp.sum(jnp.sum(masked * masked, axis=0, keepdims=True), axis=3, keepdims=True) / WINDOWS + 1e-06
                whitened = masked / jnp.sqrt(power)
                for part in range(PARTS):
                    for w in range(WINDOWS // LANES):
                        for f in range(FSUB):
                            stage[b, part, w, pl.ds(f, OWN, stride=FSUB), :] = whitened[
                                part, f, :, w * LANES:(w + 1) * LANES]
            for b in range(BATCH):
                for part in range(PARTS):
                    for w in range(WINDOWS // LANES):
                        send[k, nth(n * BATCH + b), part, :, w * LANES:(w + 1) * LANES] = stage[b, part, w].astype(jnp.bfloat16)
            for b in range(BATCH):
                put(k, nth(n * BATCH + b))
            return 0

        lax.fori_loop(0, PEERS // BATCH, body, 0)

    def wait_in(k):
        def body(s, _):
            here = jnp.logical_and(alone, s == dev)

            @pl.when(jnp.logical_not(here))
            def _():
                in_copy(k, s, s).wait_recv()

            @pl.when(here)
            def _():
                in_self(k).wait()

            return 0

        lax.fori_loop(0, PEERS, body, 0)

    def regroup(k):
        for part in range(PARTS):
            for w in range(WINDOWS // LANES):
                spread[w] = recv[k, :, part, :, w * LANES:(w + 1) * LANES].astype(jnp.float32).reshape(
                    PEERS * ROWS, LANES)
            for f in range(FSUB):
                for w in range(WINDOWS // LANES):
                    at = part * WINDOWS + w * LANES
                    blocks[k, 0, f, :, at:at + LANES] = spread[
                        w, pl.ds(f, GROUP, stride=FSUB), :].astype(jnp.bfloat16)

    def ring_copy(by, src, dst, k, which, f):
        return pltpu.make_async_remote_copy(
            src_ref=src, dst_ref=dst, send_sem=ring_send.at[k, which, f], recv_sem=ring_recv.at[k, which, f],
            device_id=ring(by), device_id_type=MESH)

    def next_copy(k, f):
        return ring_copy(1, blocks.at[k, 0, f], blocks.at[k, 1, f], k, 0, f)

    def third_copy(k, f):
        return ring_copy(3, blocks.at[k, 0, f], blocks.at[k, 2, f], k, 1, f)

    def turn_copy(k, f):
        return ring_copy(-3, blocks.at[k, 0, f], carry.at[k, f], k, 2, f)

    def pass_copy(k, f):
        return ring_copy(4, carry.at[k, f], blocks.at[k, 1, f], k, 0, f)

    def loan_copy(k):
        return ring_copy(-1, loan.at[k], back.at[k, 3], k, 3, 0)

    def send_ring(k):
        next_copy(k, FSUB - 1).start()
        for f in range(FSUB):
            if f < FSUB - 1:
                @pl.when(y < 3)
                def _():
                    next_copy(k, f).start()

                @pl.when(y == 3)
                def _():
                    turn_copy(k, f).start()

            third_copy(k, f).start()

    def pass_on(k, f):
        @pl.when(jnp.logical_and(y == 0, f < FSUB - 1))
        def _():
            turn_copy(k, f).wait_recv()
            pass_copy(k, f).start()

    def end_ring(k):
        next_copy(k, FSUB - 1).wait_send()
        for f in range(FSUB):
            if f < FSUB - 1:
                @pl.when(y < 3)
                def _():
                    next_copy(k, f).wait_send()

                @pl.when(y == 3)
                def _():
                    turn_copy(k, f).wait_send()

                @pl.when(y == 0)
                def _():
                    pass_copy(k, f).wait_send()

            third_copy(k, f).wait_send()
        loan_copy(k).wait_send()

    def cross(k, one, other, put, ready):
        def body(f, _):
            ready(f)
            own = blocks[k, one, f]
            left[0:GROUP, :] = own
            left[GROUP:, 0:WINDOWS] = own[:, WINDOWS:]
            left[GROUP:, WINDOWS:] = -own[:, :WINDOWS]
            product = lax.dot_general(
                left[...], blocks[k, other, f], (((1,), (1,)), ((), ())), preferred_element_type=jnp.float32)
            for part in range(PARTS):
                terms[pl.ds(part * FSUB + f, GROUP, stride=PARTS * FSUB), :] = product[
                    part * GROUP:(part + 1) * GROUP]
            return 0

        lax.fori_loop(0, FSUB, body, 0)
        put[...] = terms[...].astype(jnp.bfloat16).reshape(PEERS, BACK_ROWS, LANES)

    def out_refs(k, late, s, place, c):
        first, last = BATCHES[k][late]
        return back.at[k, first:last, s], home.at[k, place, c, first:last]

    def out_copy(k, late, n):
        s, place, target, here = route(n)
        src, dst = out_refs(k, late, s, place, core)
        far = pltpu.make_async_remote_copy(
            src_ref=src, dst_ref=dst, send_sem=back_send.at[k, late, n],
            recv_sem=back_recv.at[k, late, place, core], device_id=target, device_id_type=MESH)
        return here, far, pltpu.make_async_copy(src, dst, back_recv.at[k, late, place, core])

    def send_out(k, late):
        def body(n, _):
            here, far, near = out_copy(k, late, n)

            @pl.when(jnp.logical_not(here))
            def _():
                far.start()

            @pl.when(here)
            def _():
                near.start()

            return 0

        lax.fori_loop(0, PEERS, body, 0)

    def wait_out(k, late, lowest, highest):
        def body(n, _):
            place, c = n // 2, n % 2

            @pl.when(place != unused)
            def _():
                _, dst = out_refs(k, late, 0, place, c)
                pltpu.make_async_copy(dst, dst, back_recv.at[k, late, place, c]).wait()

            return 0

        lax.fori_loop(2 * lowest, 2 * highest, body, 0)

    scale = 1.0 / np.sqrt(np.float32(WINDOWS) * FREQS)

    def lags(k, lowest, count, start, slot, pair):
        rows = pl.multiple_of(pair * 16, 16)
        values = home[k, lowest:lowest + count, :, slot, pl.ds(rows, 16), :].reshape(count * PLANE_ROWS, LANES)
        window = pl.ds(pl.multiple_of((start + PLANES) % PLANES * PLANE_ROWS, PLANE_ROWS), count * PLANE_ROWS)
        both = lax.dot_general(
            values, table_ref[k, window, :], (((0,), (0,)), ((), ())), preferred_element_type=jnp.float32)
        return (both[:, :2 * LAGS] + both[:, 2 * LAGS:]) * scale

    def reach_lags(k, side, slot, pair):
        return lags(k, side * REACH, REACH, plane - side * (REACH - 1), slot, pair)

    def gather_first():
        def body(n, _):
            slot, pair = n // 2, n % 2
            for side in range(2):
                values = reach_lags(0, side, slot, pair)
                for c in range(2):
                    sums[side, slot, pair * 2 + c] = values[:, c * LAGS:(c + 1) * LAGS]
            return 0

        lax.fori_loop(0, ROUNDS * 2, body, 0)

    def part_copy(side, slot):
        goal = (plane + (2 * side - 1) * HOP + PLANES) % PLANES
        return pltpu.make_async_remote_copy(
            src_ref=part.at[side, slot], dst_ref=got.at[side, slot], send_sem=part_send.at[side, slot],
            recv_sem=part_recv.at[side, slot], device_id=at_plane(goal), device_id_type=MESH)

    def gather_last(slot):
        def body(pair, _):
            for side in range(2):
                values = reach_lags(1, side, slot, pair)
                for c in range(2):
                    total = sums[side, slot, pair * 2 + c] + values[:, c * LAGS:(c + 1) * LAGS]
                    part[side, slot, pair * 2 + c] = total.astype(jnp.bfloat16)
            return 0

        lax.fori_loop(0, 2, body, 0)
        for side in range(2):
            part_copy(side, slot).start()

    def round_of(slot):
        return (0, 1, 3, 2)[slot]

    def near_lags(slot):
        def body(pair, _):
            values = lags(0, 2 * REACH, NEAR, plane - 1, slot, pair) + lags(1, 2 * REACH, NEAR, plane - 1, slot, pair)
            for c in range(2):
                out_ref[round_of(slot), pair * 2 + c] = values[:, c * LAGS:(c + 1) * LAGS]
            return 0

        lax.fori_loop(0, 2, body, 0)

    def add_parts(slot):
        def body(c, _):
            out_ref[round_of(slot), c] += got[0, slot, c].astype(jnp.float32) + got[1, slot, c].astype(jnp.float32)
            return 0

        lax.fori_loop(0, OWN, body, 0)

    def end_in(k):
        def body(n, _):
            @pl.when(jnp.logical_not(jnp.logical_and(alone, n == chunk)))
            def _():
                in_copy(k, n, dev).wait_send()

            return 0

        lax.fori_loop(0, PEERS, body, 0)

    def end_out(k, late):
        def body(n, _):
            here, far, _ = out_copy(k, late, n)

            @pl.when(jnp.logical_not(here))
            def _():
                far.wait_send()

            return 0

        lax.fori_loop(0, PEERS, body, 0)

    load_x(0).wait()
    targets = 2 * PEERS + 7 - 2 * (x == 0).astype(jnp.int32) - 2 * (x == 2).astype(jnp.int32)
    pl.semaphore_wait(barrier, targets)
    send_in(0)
    load_x(1).wait()
    send_in(1)
    for k in range(SUB):
        wait_in(k)
        regroup(k)
        send_ring(k)
        cross(k, 0, 0, back.at[k, 0], lambda f: pass_on(k, f))
        if k > 0:
            send_out(k, 0)
        end_in(k)
        cross(k, 0, 1, back.at[k, 1], lambda f: next_copy(k, f).wait_recv())
        if k > 0:
            send_out(k, 1)
        for f in range(FSUB):
            third_copy(k, f).wait_recv()
        cross(k, 1, 2, loan.at[k], lambda f: None)
        loan_copy(k).start()
        cross(k, 0, 2, back.at[k, 2], lambda f: None)
        if k > 0:
            send_out(k, 2)
        loan_copy(k).wait_recv()
        send_out(k, len(BATCHES[k]) - 1)
    load_table.wait()
    for k in range(SUB):
        home[k, unused] = jnp.zeros((2, ROUNDS, BACK_ROWS, LANES), jnp.bfloat16)
    wait_out(0, 0, 0, 2 * REACH)
    gather_first()
    for late in range(len(BATCHES[0])):
        wait_out(0, late, 2 * REACH, PLACES)
        end_out(0, late)
    end_ring(0)
    for slot in range(ROUNDS):
        wait_out(1, slot, 0, 2 * REACH)
        gather_last(slot)
        wait_out(1, slot, 2 * REACH, PLACES)
        near_lags(slot)
        end_out(1, slot)
    end_ring(1)
    for slot in range(ROUNDS):
        for side in range(2):
            part_copy(side, slot).wait_recv()
        add_parts(slot)
    for slot in range(ROUNDS):
        for side in range(2):
            part_copy(side, slot).wait_send()


def local(spectra, validity):
    table = jnp.asarray(lag_table())
    vmem = pl.BlockSpec(memory_space=pltpu.VMEM)
    main = pl.BlockSpec(memory_space=pltpu.HBM)
    dma = pltpu.SemaphoreType.DMA
    return pl.pallas_call(
        kernel,
        out_shape=jax.ShapeDtypeStruct((ROUNDS, OWN, GROUP, LAGS), jnp.float32),
        in_specs=[main, vmem, main],
        out_specs=vmem,
        scratch_shapes=[
            pltpu.VMEM((PARTS, FREQS, OWN, WINDOWS), jnp.bfloat16),
            pltpu.VMEM((SUB, (PLANES + REACH - 1) * PLANE_ROWS, 4 * LANES), jnp.bfloat16),
            pltpu.VMEM((BATCH, PARTS, WINDOWS // LANES, ROWS, LANES), jnp.float32),
            pltpu.VMEM((SUB, PEERS, PARTS, ROWS, WINDOWS), jnp.bfloat16),
            pltpu.VMEM((SUB, PEERS, PARTS, ROWS, WINDOWS), jnp.bfloat16),
            pltpu.VMEM((WINDOWS // LANES, PEERS * ROWS, LANES), jnp.float32),
            pltpu.VMEM((SUB, 3, FSUB, GROUP, PARTS * WINDOWS), jnp.bfloat16),
            pltpu.VMEM((SUB, FSUB, GROUP, PARTS * WINDOWS), jnp.bfloat16),
            pltpu.VMEM((2 * GROUP, PARTS * WINDOWS), jnp.bfloat16),
            pltpu.VMEM((GROUP * PARTS * FSUB, LANES), jnp.float32),
            pltpu.VMEM((SUB, PEERS, BACK_ROWS, LANES), jnp.bfloat16),
            pltpu.VMEM((SUB, ROUNDS, PEERS, BACK_ROWS, LANES), jnp.bfloat16),
            pltpu.VMEM((SUB, PLACES, 2, ROUNDS, BACK_ROWS, LANES), jnp.bfloat16),
            pltpu.VMEM((2, ROUNDS, OWN, GROUP, LAGS), jnp.float32),
            pltpu.VMEM((2, ROUNDS, OWN, GROUP, LAGS), jnp.bfloat16),
            pltpu.VMEM((2, ROUNDS, OWN, GROUP, LAGS), jnp.bfloat16),
            dma((SUB, PEERS)), dma((SUB, PEERS)),
            dma((SUB, 4, FSUB)), dma((SUB, 4, FSUB)),
            dma((SUB, ROUNDS, PEERS)), dma((SUB, ROUNDS, PLACES, 2)),
            dma((2, ROUNDS)), dma((2, ROUNDS)),
            dma((SUB,)), dma((SUB + 1,)),
        ],
        compiler_params=pltpu.CompilerParams(
            collective_id=1, has_side_effects=True, vmem_limit_bytes=54 << 20),
        name="correlate",
    )(spectra, validity, table)


def solution(mesh):
    in_specs = (P(None, None, ("grp", "dev"), None), P(("grp", "dev"), None))
    out_specs = P(None, ("grp", "dev"), None, None)
    return jax.shard_map(local, mesh=mesh, in_specs=in_specs, out_specs=out_specs, check_vma=False)
```
